512 devices in a mesh: ctx: 64 (over y, x, core), head: 8 (over z).
Axes of the slice: x: 4, y: 8, z: 8, core: 2. Of those that a mesh axis runs over, the one named last changes fastest.
Arguments:
- queries: bfloat16 [16384, 2048], P('ctx', 'head'), may hold values from -160 to 160
- keys: bfloat16 [16384, 2048], P('ctx', 'head'), may hold values from -6 to 6
- values: bfloat16 [16384, 2048], P('ctx', 'head'), may hold values from -6 to 6
- group_lens: int32 [32], replicated, may hold values from 1 to 1024, 16384 in all
- dispatch: int32 [256], replicated, may hold values from 0 to 255, each once
- out_weight: bfloat16 [2048, 3072], P('head'), may hold values from -0.125 to 0.125
Outputs:
- mixed: bfloat16 [16384, 3072], P(('ctx', 'head'))
The draws below stay inside these ranges and needn't reach their ends.
Inputs may be any that keep to these rules, and one draw needn't show every extreme that they name: `dispatch`: each slice number appears once. `group_lens`: positive, summing to 16384, the largest exactly 1024.
All inputs are finite; a program needn't handle non-finite values.
Results may differ from the reference program's by a relative error of at most 0.02.
Values may be sent and summed in bfloat16 or wider, within the bound.
A program may use at most 128 MiB of HBM per device.

```python
import math
import jax
import jax.numpy as jnp
import numpy as np
from jax import lax

D = 3072
HEADS = 16
HEAD_DIM = 128
SLICE = 64
NCHUNK = 32
TOKENS = 16384
NSLICES = 256
MOST = 1024


def base_keys(key):
    shape = (TOKENS, HEADS * HEAD_DIM)
    keys = jax.random.normal(jax.random.fold_in(key, 1), shape, jnp.float32)
    return keys


def draw_keys(key, part):
    keys = base_keys(key)
    result = jnp.clip(keys, -6.0, 6.0)
    return result.astype(jnp.bfloat16)


def draw_queries(key, part):
    key = jax.random.fold_in(key, 11)
    fresh = jnp.clip(jax.random.normal(key, (TOKENS, HEADS * HEAD_DIM), jnp.float32), -6.0, 6.0)
    result = fresh
    return result.astype(jnp.bfloat16)


def levels(rng, dims, shards, low, largest):
    def one(position, parts):
        steps = jax.random.uniform(jax.random.fold_in(jax.random.fold_in(rng, 6), position), (parts,), jnp.float32, low / len(shards), largest / len(shards))
        return jnp.repeat(jnp.exp(steps), dims[position] // parts).reshape((-1,) + (1,) * (len(dims) - position - 1))

    factor_of = one(*shards[0])
    for cut in shards[1:]:
        factor_of = factor_of * one(*cut)
    return factor_of


def length_profile(count, total, most, skew):
    loads = [(1 << 20) // math.isqrt(grade ** skew) + 1 for grade in range(2, count + 1)]
    rest, counts = total - most - (count - 1), [1] * (count - 1)
    while rest > 0:
        free = [i for i in range(count - 1) if counts[i] < most]
        mass, left = sum([loads[i] for i in free]), rest
        for i in free:
            more = min(most - counts[i], max(1, left * loads[i] // mass), rest)
            counts[i] = counts[i] + more
            rest = rest - more
    return np.array([most] + counts)


def ragged(own_key, amount, total, reach, skew):
    if amount == 2:
        one = jax.random.randint(own_key, (), max(1, total - reach), min(reach, total - 1) + 1)
        return jnp.stack([one, total - one])
    tallies = jnp.asarray(length_profile(amount, total, reach, skew), jnp.int32)
    couples = (amount - 1) // 2
    source_of, sink = tallies[1:1 + 2 * couples:2], tallies[2:2 + 2 * couples:2]
    room = jnp.minimum(source_of - 1, reach - sink)
    shifted = jax.random.randint(jax.random.fold_in(own_key, 1), (couples,), 0, 1 << 20) % (room + 1)
    tallies = tallies.at[1:1 + 2 * couples:2].set(source_of - shifted).at[2:2 + 2 * couples:2].set(sink + shifted)
    return tallies[jax.random.permutation(jax.random.fold_in(own_key, 2), amount)]


def bell_draw(key, dims, scale, most, split=(), held_as=jnp.bfloat16):
    values = scale * jax.random.normal(key, dims, jnp.float32)
    if split:
        values = values * levels(key, dims, split, -0.22, 0.18)
    return jnp.clip(values, -most, most).astype(held_as)


def setup_inputs(seed: int = 0) -> dict:
    seeds = jax.random.split(jax.random.key(seed), 7)
    queries = draw_queries(jax.random.fold_in(seeds[6], 71), 0)
    keys = draw_keys(jax.random.fold_in(seeds[6], 71), 0)
    values = bell_draw(seeds[2], (TOKENS, HEADS * HEAD_DIM), 1.0, 6.0, ((0, 64), (1, 8)))
    group_lens = ragged(seeds[3], NCHUNK, TOKENS, MOST, 2).astype(jnp.int32)
    dispatch = jax.random.permutation(seeds[4], NSLICES).astype(jnp.int32)
    out_weight = bell_draw(seeds[5], (HEADS * HEAD_DIM, D), (HEADS * HEAD_DIM) ** -0.5, 0.125, ((0, 8),))
    return {"queries": queries, "keys": keys, "values": values, "group_lens": group_lens, "dispatch": dispatch, "out_weight": out_weight}


def group_numbers(dispatch, group_lens):
    group_ends = jnp.cumsum(group_lens)
    positions = (dispatch[:, None] * SLICE + jnp.arange(SLICE, dtype=jnp.int32)[None, :]).reshape(-1)
    return jnp.sum((group_ends[None, :] <= positions[:, None]).astype(jnp.int32), axis=1)


def reference(queries, keys, values, group_lens, dispatch, out_weight):
    token_groups = group_numbers(dispatch, group_lens)
    scale = HEAD_DIM ** -0.5
    head_queries = queries.reshape(TOKENS, HEADS, HEAD_DIM).transpose(1, 0, 2)
    head_keys = keys.reshape(TOKENS, HEADS, HEAD_DIM).transpose(1, 0, 2)
    head_values = values.reshape(TOKENS, HEADS, HEAD_DIM).transpose(1, 0, 2)
    block_size = math.gcd(TOKENS, 1024)
    block_count = TOKENS // block_size

    def one_head(operands):
        query_head, key_head, value_head = operands
        query_blocks = query_head.reshape(block_count, block_size, HEAD_DIM)
        group_blocks = token_groups.reshape(block_count, block_size)

        def one_block(pair):
            query_block, group_block = pair
            scores = jnp.dot(query_block, key_head.T, preferred_element_type=jnp.float32) * scale
            allowed = token_groups[None, :] <= group_block[:, None]
            masked = jnp.where(allowed, scores, -1.0e30)
            peak = jnp.max(masked, axis=1)
            weights = jnp.where(allowed, jnp.exp(scores - peak[:, None]), 0.0)
            total = jnp.sum(weights, axis=1)
            summed = jnp.dot(weights.astype(jnp.bfloat16), value_head, preferred_element_type=jnp.float32)
            return summed / total[:, None]

        return lax.map(one_block, (query_blocks, group_blocks)).reshape(TOKENS, HEAD_DIM)

    head_outputs = lax.map(one_head, (head_queries, head_keys, head_values))
    attended = head_outputs.transpose(1, 0, 2).reshape(TOKENS, HEADS * HEAD_DIM).astype(jnp.bfloat16)
    return jnp.dot(attended, out_weight, preferred_element_type=jnp.float32).astype(jnp.bfloat16)
```

```python
import functools

import jax
import jax.numpy as jnp
from jax import lax
from jax.experimental import pallas as pl
from jax.experimental.pallas import tpu as pltpu
from jax.sharding import PartitionSpec as P

HD = 128
SLICE = 64
NX, NY, NZ = 4, 8, 8
ROWS = 256
PIECE = 128
KEYS = NX * 2 * ROWS
D = 3072
HIDDEN = -1e30
LOG2E = 1.4426950408889634
SCALE = HD**-0.5 * LOG2E
MESH = pl.DeviceIdType.MESH


def kernel(
    lens, disp, q_in, k_in, v_in, w_in, out,
    qbuf, qbias, kbuf, vbuf, konehot, score, part_o, part_l,
    yo_send, yl_send, yo_recv, yl_recv, att, att_send, wbuf, proj, z_send, z_recv,
    loc_sem, sib_s, sib_r, q_s, q_r, kv_s, kv_r, yo_s, yo_r, yl_s, yl_r, at_s, at_r, z_s, z_r,
):
    ctx, z = lax.axis_index("ctx"), lax.axis_index("head")
    c = lax.rem(ctx, 2)
    x = lax.rem(ctx // 2, NX)
    y = ctx // (2 * NX)

    def at(yy, xx, cc, zz):
        return ((yy * NX + xx) * 2 + cc, zz)

    def ring(i, step, size):
        return lax.rem(i + step + size, size)

    sibling = at(y, x, 1 - c, z)

    def y_dev(step):
        return at(ring(y, step, NY), x, c, z)

    def x_dev(step):
        return at(y, ring(x, step, NX), c, z)

    def z_dev(step):
        return at(y, x, c, ring(z, step, NZ))

    partners = [sibling] + [f(s) for f in (x_dev, y_dev, z_dev) for s in (-1, 1)]
    barrier = pltpu.get_barrier_semaphore()
    for dev in partners:
        pl.semaphore_signal(barrier, inc=1, device_id=dev, device_id_type=MESH)
    pl.semaphore_wait(barrier, len(partners))

    sent = []

    def send(src, dst, s, r, dev):
        copy = pltpu.make_async_remote_copy(
            src_ref=src, dst_ref=dst, send_sem=s, recv_sem=r, device_id=dev, device_id_type=MESH
        )
        copy.start()
        sent.append(copy)
        return copy

    mine = pl.ds(pl.multiple_of(c * HD, HD), HD)
    other = pl.ds(pl.multiple_of((1 - c) * HD, HD), HD)
    swaps = [
        send(q_in.at[:, p, :, other], qbuf.at[y, p, c], sib_s.at[p], sib_r.at[p], sibling)
        for p in range(2)
    ]
    swaps.append(send(k_in.at[:, other], kbuf.at[x, c], sib_s.at[2], sib_r.at[2], sibling))
    swaps.append(send(v_in.at[:, other], vbuf.at[x, c], sib_s.at[3], sib_r.at[3], sibling))
    local = [
        pltpu.make_async_copy(q_in.at[:, p, :, mine], qbuf.at[y, p, c], loc_sem.at[p])
        for p in range(2)
    ]
    local.append(pltpu.make_async_copy(k_in.at[:, mine], kbuf.at[x, c], loc_sem.at[2]))
    local.append(pltpu.make_async_copy(v_in.at[:, mine], vbuf.at[x, c], loc_sem.at[3]))
    local.append(pltpu.make_async_copy(w_in, wbuf, loc_sem.at[4]))
    for copy in local:
        copy.start()
    for copy in swaps:
        copy.wait_recv()
    for copy in local[:4]:
        copy.wait()

    left, right = 0, 1

    def q_send(slot, owner, dev, piece=None):
        ref = qbuf.at[owner] if piece is None else qbuf.at[owner, piece]
        return send(ref, ref, q_s.at[slot], q_r.at[slot], dev)

    def kv_send(slot, ref, owner, dev):
        return send(ref.at[owner], ref.at[owner], kv_s.at[slot], kv_r.at[slot], dev)

    q_hop = [q_send(0, y, y_dev(1)), q_send(1, y, y_dev(-1))]
    kv_hop = [
        kv_send(0, kbuf, x, x_dev(1)),
        kv_send(1, vbuf, x, x_dev(-1)),
        kv_send(2, vbuf, x, x_dev(1)),
        kv_send(3, kbuf, x, x_dev(-1)),
    ]

    lane = lax.broadcasted_iota(jnp.int32, (1, HD), 1)

    def bounds(g, carry):
        total, first, last = carry
        after = total + lens[g]
        return after, jnp.where(lane == g, total, first), jnp.where(lane == g, after, last)

    _, first, last = lax.fori_loop(
        0, 32, bounds,
        (jnp.int32(0), jnp.full((1, HD), -1, jnp.int32), jnp.zeros((1, HD), jnp.int32)),
    )
    sub64 = lax.broadcasted_iota(jnp.int32, (SLICE, HD), 0)
    sub16 = lax.broadcasted_iota(jnp.int32, (16, HD), 0)

    def key_marks(s, _):
        pos = disp[y * (KEYS // SLICE) + s] * SLICE + sub64
        inside = jnp.where((first <= pos) & (pos < last), 1.0, 0.0)
        konehot[pl.ds(pl.multiple_of(s * SLICE, SLICE), SLICE), :] = inside.astype(jnp.bfloat16)
        return 0

    lax.fori_loop(0, KEYS // SLICE, key_marks, 0)

    def query_marks(i, _):
        owner, half, s = i // 8, lax.rem(i // 4, 2), lax.rem(i, 4)
        start = disp[(owner * NX + x) * 8 + half * 4 + s] * SLICE
        for j in range(2):
            for p in range(2):
                pos = start + (j * 32 + p * 16) + sub16
                qbias[owner, p, half, 2 * s + j] = jnp.where(first > pos, HIDDEN, 0.0).astype(
                    jnp.bfloat16
                )
        return 0

    lax.fori_loop(0, NY * 8, query_marks, 0)

    q_hop[0].wait_recv()
    q_hop.append(q_send(2, ring(y, -1, NY), y_dev(1)))
    q_hop[1].wait_recv()
    q_hop.append(q_send(3, ring(y, 1, NY), y_dev(-1)))
    kv_hop[0].wait_recv()
    kv_hop.append(kv_send(4, kbuf, ring(x, -1, NX), x_dev(1)))
    kv_hop[1].wait_recv()
    kv_hop.append(kv_send(5, vbuf, ring(x, 1, NX), x_dev(-1)))
    q_hop[2].wait_recv()
    q_hop.append(q_send(4, ring(y, -2, NY), y_dev(1)))
    q_hop[3].wait_recv()
    q_hop.append(q_send(5, ring(y, 2, NY), y_dev(-1)))
    for i in (2, 3, 4, 5):
        kv_hop[i].wait_recv()
    q_hop[4].wait_recv()
    q_hop.append(q_send(6, ring(y, -3, NY), y_dev(1), 0))
    q_hop[5].wait_recv()
    q_hop.append(q_send(7, ring(y, 3, NY), y_dev(-1), 1))

    ones = jnp.ones((512, HD), jnp.bfloat16)

    def attend(owner, p):
        rows = 2 * PIECE
        qa = jnp.concatenate(
            [qbuf[owner, p].reshape(rows, HD), qbias[owner, p].reshape(rows, HD)], axis=1
        )
        peak = None
        for b in range(NX):
            ka = jnp.concatenate(
                [kbuf[b].reshape(512, HD), konehot[b * 512 : (b + 1) * 512, :]], axis=1
            )
            s = lax.dot_general(
                qa, ka, (((1,), (1,)), ((), ())), preferred_element_type=jnp.float32
            )
            score[:, b * 512 : (b + 1) * 512] = s
            for t in range(4):
                tile = s[:, t * HD : (t + 1) * HD]
                peak = tile if peak is None else jnp.maximum(peak, tile)
        peak = jnp.max(peak, axis=1, keepdims=True)
        total = jnp.zeros((rows, 2 * HD), jnp.float32)
        for b in range(NX):
            w = jnp.exp2((score[:, b * 512 : (b + 1) * 512] - peak) * SCALE).astype(jnp.bfloat16)
            va = jnp.concatenate([vbuf[b].reshape(512, HD), ones], axis=1)
            total = total + jnp.dot(w, va, preferred_element_type=jnp.float32)
        weight = total[:, HD:]
        part_o[owner, p] = total[:, :HD] / weight
        part_l[owner, p] = jnp.log2(weight) + peak * SCALE

    def attend_step(j):
        def one(i, _):
            p, short = i // 2, lax.rem(i, 2)
            way = (2 * p - 1) * (1 - 2 * short)
            attend(ring(y, way * (5 - j - short), NY), p)
            return 0

        lax.fori_loop(0, 4, one, 0)

    def merge(o, l, slot):
        box = yl_recv[slot]
        column = jnp.concatenate(
            [
                jnp.transpose(jnp.broadcast_to(box[4 * h : 4 * h + 1, :], (HD, HD)))
                for h in range(2)
            ],
            axis=0,
        )
        top = jnp.maximum(l, column)
        a, b = jnp.exp2(l - top), jnp.exp2(column - top)
        total = a + b
        o = (o * a + yo_recv[slot].astype(jnp.float32) * b) / total
        return o, top + jnp.log2(total)

    sub8 = lax.broadcasted_iota(jnp.int32, (8, HD), 0)

    def y_send(p, slot, o, l, dev):
        i = p * 7 + slot
        yo_send[i] = o.astype(jnp.bfloat16)
        halves = [jnp.transpose(l[h * HD : (h + 1) * HD, :])[:8, :] for h in range(2)]
        yl_send[i] = jnp.where(sub8 < 4, halves[0], halves[1])
        return (
            send(yo_send.at[i], yo_recv.at[i], yo_s.at[i], yo_r.at[i], dev),
            send(yl_send.at[i], yl_recv.at[i], yl_s.at[i], yl_r.at[i], dev),
        )

    hops = {}
    for copy in q_hop[6:]:
        copy.wait_recv()
    for j in range(1, 5):
        attend_step(j)
        for p in range(2):
            way = 2 * p - 1
            for short in range(2):
                if short and j == 4:
                    continue
                travel = -way if short else way
                owner = ring(y, travel * (5 - j - short), NY)
                o, l = part_o[owner, p], part_l[owner, p]
                slot = 4 * short + j - 1
                if j > 1:
                    for copy in hops[p, slot - 1]:
                        copy.wait_recv()
                    o, l = merge(o, l, p * 7 + slot - 1)
                hops[p, slot] = y_send(p, slot, o, l, y_dev(travel))

    swaps = []
    for p in range(2):
        o, l = part_o[y, p], part_l[y, p]
        for slot in (6, 3):
            for copy in hops[p, slot]:
                copy.wait_recv()
            o, l = merge(o, l, p * 7 + slot)
        o = o.astype(jnp.bfloat16)
        keep = jnp.where(c == 0, o[:PIECE], o[PIECE:])
        give = jnp.where(c == 0, o[PIECE:], o[:PIECE])
        att_send[p] = give
        swaps.append(send(att_send.at[p], att.at[p, c], at_s.at[p], at_r.at[p], sibling))
        att[p, c] = keep

    local[4].wait()

    def project(p):
        a = jnp.concatenate([att[p, 0], att[p, 1]], axis=1)

        def columns(n, _):
            cut = pl.ds(pl.multiple_of(n * 768, 768), 768)
            r = jnp.dot(a, wbuf[:, cut], preferred_element_type=jnp.float32)
            proj[p, :, :, cut] = r.reshape(NZ, 16, 768)
            return 0

        lax.fori_loop(0, D // 768, columns, 0)

    zhops = {}
    for j in range(1, 5):
        for p in range(2):
            if j == 1:
                swaps[p].wait_recv()
                project(p)
            way = 2 * p - 1
            for short in range(2):
                if short and j == 4:
                    continue
                travel = -way if short else way
                owner = ring(z, travel * (5 - j - short), NZ)
                r = proj[p, owner]
                slot = 4 * short + j - 1
                i = p * 7 + slot
                if j > 1:
                    zhops[p, slot - 1].wait_recv()
                    r = r + z_recv[i - 1].astype(jnp.float32)
                z_send[i] = r.astype(jnp.bfloat16)
                zhops[p, slot] = send(
                    z_send.at[i], z_recv.at[i], z_s.at[i], z_r.at[i], z_dev(travel)
                )
    for p in range(2):
        r = proj[p, z]
        for slot in (6, 3):
            zhops[p, slot].wait_recv()
            r = r + z_recv[p * 7 + slot].astype(jnp.float32)
        out[p * 16 : (p + 1) * 16, :] = r.astype(jnp.bfloat16)
    for copy in sent:
        copy.wait_send()


def body(queries, keys, values, group_lens, dispatch, out_weight):
    bf, f32 = jnp.bfloat16, jnp.float32
    dma = pltpu.SemaphoreType.DMA
    anywhere = pl.BlockSpec(memory_space=pl.ANY)
    smem = pl.BlockSpec(memory_space=pltpu.SMEM)
    return pl.pallas_call(
        kernel,
        out_shape=jax.ShapeDtypeStruct((ROWS // NZ, D), bf),
        in_specs=[smem, smem, anywhere, anywhere, anywhere, anywhere],
        out_specs=pl.BlockSpec(memory_space=pltpu.VMEM),
        scratch_shapes=[
            pltpu.VMEM((NY, 2, 2, NZ, 16, HD), bf),
            pltpu.VMEM((NY, 2, 2, NZ, 16, HD), bf),
            pltpu.VMEM((NX, 2, ROWS, HD), bf),
            pltpu.VMEM((NX, 2, ROWS, HD), bf),
            pltpu.VMEM((KEYS, HD), bf),
            pltpu.VMEM((2 * PIECE, KEYS), f32),
            pltpu.VMEM((NY, 2, 2 * PIECE, HD), f32),
            pltpu.VMEM((NY, 2, 2 * PIECE, HD), f32),
            pltpu.VMEM((14, 2 * PIECE, HD), bf),
            pltpu.VMEM((14, 8, HD), f32),
            pltpu.VMEM((14, 2 * PIECE, HD), bf),
            pltpu.VMEM((14, 8, HD), f32),
            pltpu.VMEM((2, 2, PIECE, HD), bf),
            pltpu.VMEM((2, PIECE, HD), bf),
            pltpu.VMEM((2 * HD, D), bf),
            pltpu.VMEM((2, NZ, 16, D), f32),
            pltpu.VMEM((14, 16, D), bf),
            pltpu.VMEM((14, 16, D), bf),
            dma((5,)), dma((4,)), dma((4,)), dma((8,)), dma((8,)), dma((6,)), dma((6,)),
            dma((14,)), dma((14,)), dma((14,)), dma((14,)), dma((2,)), dma((2,)),
            dma((14,)), dma((14,)),
        ],
        compiler_params=pltpu.CompilerParams(
            collective_id=0, has_side_effects=True, vmem_limit_bytes=48 * 1024 * 1024
        ),
        cost_estimate=pl.CostEstimate(
            flops=9_000_000_000, bytes_accessed=6_000_000, transcendentals=8_400_000
        ),
    )(
        group_lens,
        dispatch,
        queries.reshape(NZ, 2, 16, 2 * HD),
        keys,
        values,
        out_weight,
    )


def solution(mesh):
    return jax.shard_map(
        body,
        mesh=mesh,
        in_specs=(P("ctx", "head"), P("ctx", "head"), P("ctx", "head"), P(), P(), P("head", None)),
        out_specs=P(("ctx", "head"), None),
        check_vma=False,
    )
```

```python
import functools

import jax
import jax.numpy as jnp
from jax import lax
from jax.experimental import pallas as pl
from jax.experimental.pallas import tpu as pltpu
from jax.sharding import PartitionSpec as P

HD = 128
SLICE = 64
NX, NY, NZ = 4, 8, 8
ROWS = 256
PIECE = 128
KEYS = NX * 2 * ROWS
D = 3072
HIDDEN = -1e30
LOG2E = 1.4426950408889634
SCALE = HD**-0.5 * LOG2E
MESH = pl.DeviceIdType.MESH


def kernel(
    lens, disp, q_in, k_in, v_in, w_in, out,
    qbuf, qbias, kbuf, vbuf, vt, konehot, score_a, score_b, peak_a, peak_b,
    part_o, part_l, yo_send, yl_send, yo_recv, yl_recv, att, att_send, wbuf, proj, z_send, z_recv,
    loc_sem, sib_s, sib_r, q_s, q_r, kv_s, kv_r, yo_s, yo_r, yl_s, yl_r, at_s, at_r, z_s, z_r,
):
    ctx, z = lax.axis_index("ctx"), lax.axis_index("head")
    c = lax.rem(ctx, 2)
    x = lax.rem(ctx // 2, NX)
    y = ctx // (2 * NX)

    def at(yy, xx, cc, zz):
        return ((yy * NX + xx) * 2 + cc, zz)

    def ring(i, step, size):
        return lax.rem(i + step + size, size)

    sibling = at(y, x, 1 - c, z)

    def y_dev(step):
        return at(ring(y, step, NY), x, c, z)

    def x_dev(step):
        return at(y, ring(x, step, NX), c, z)

    def z_dev(step):
        return at(y, x, c, ring(z, step, NZ))

    partners = [sibling, y_dev(4)] + [f(s) for f in (x_dev, y_dev, z_dev) for s in (-1, 1)]
    barrier = pltpu.get_barrier_semaphore()
    for dev in partners:
        pl.semaphore_signal(barrier, inc=1, device_id=dev, device_id_type=MESH)

    mine = pl.ds(pl.multiple_of(c * HD, HD), HD)
    other = pl.ds(pl.multiple_of((1 - c) * HD, HD), HD)
    local = [
        pltpu.make_async_copy(q_in.at[:, p, :, mine], qbuf.at[0, p, c], loc_sem.at[p])
        for p in range(2)
    ]
    local.append(pltpu.make_async_copy(k_in.at[:, mine], kbuf.at[0, c], loc_sem.at[2]))
    local.append(pltpu.make_async_copy(v_in.at[:, mine], vbuf.at[0, c], loc_sem.at[3]))
    load_w = pltpu.make_async_copy(w_in, wbuf, loc_sem.at[4])
    for copy in local:
        copy.start()
    pl.semaphore_wait(barrier, len(partners))

    sent = []

    def send(src, dst, s, r, dev):
        copy = pltpu.make_async_remote_copy(
            src_ref=src, dst_ref=dst, send_sem=s, recv_sem=r, device_id=dev, device_id_type=MESH
        )
        copy.start()
        sent.append(copy)
        return copy

    swaps = [
        send(k_in.at[:, other], kbuf.at[0, c], sib_s.at[2], sib_r.at[2], sibling),
        send(v_in.at[:, other], vbuf.at[0, c], sib_s.at[3], sib_r.at[3], sibling),
    ] + [
        send(q_in.at[:, p, :, other], qbuf.at[0, p, c], sib_s.at[p], sib_r.at[p], sibling)
        for p in range(2)
    ]
    for copy in local:
        copy.wait()
    for copy in swaps:
        copy.wait_recv()

    def q_send(slot, block, step, piece):
        there = (block - step) % NY
        return send(
            qbuf.at[block, piece], qbuf.at[there, piece], q_s.at[slot], q_r.at[slot], y_dev(step)
        )

    def kv_send(slot, ref, block, step):
        there = (block - step) % NX
        return send(ref.at[block], ref.at[there], kv_s.at[slot], kv_r.at[slot], x_dev(step))

    k_right = kv_send(0, kbuf, 0, 1)
    v_left = kv_send(1, vbuf, 0, -1)
    hop = {}
    for p in range(2):
        for w in range(2):
            hop[1, p, w] = q_send(2 * p + w, 0, 1 - 2 * w, p)
    v_right = kv_send(2, vbuf, 0, 1)
    k_left = kv_send(3, kbuf, 0, -1)
    across = [q_send(12 + p, 0, 4, p) for p in range(2)]
    load_w.start()

    lane = lax.broadcasted_iota(jnp.int32, (1, HD), 1)

    def bounds(g, carry):
        total, first, last = carry
        after = total + lens[g]
        return after, jnp.where(lane == g, total, first), jnp.where(lane == g, after, last)

    _, first, last = lax.fori_loop(
        0, 32, bounds,
        (jnp.int32(0), jnp.full((1, HD), -1, jnp.int32), jnp.zeros((1, HD), jnp.int32)),
    )
    sub64 = lax.broadcasted_iota(jnp.int32, (SLICE, HD), 0)
    sub16 = lax.broadcasted_iota(jnp.int32, (16, HD), 0)

    def key_marks(s, _):
        block = ring(x, s // 8, NX)
        pos = disp[(y * NX + block) * 8 + lax.rem(s, 8)] * SLICE + sub64
        inside = jnp.where((first <= pos) & (pos < last), 1.0, 0.0)
        konehot[pl.ds(pl.multiple_of(s * SLICE, SLICE), SLICE), :] = inside.astype(jnp.bfloat16)
        return 0

    lax.fori_loop(0, KEYS // SLICE, key_marks, 0)

    def query_marks(i, _):
        owner, half, s = i // 8, lax.rem(i // 4, 2), lax.rem(i, 4)
        start = disp[(ring(y, owner, NY) * NX + x) * 8 + half * 4 + s] * SLICE
        for j in range(2):
            for p in range(2):
                pos = start + (j * 32 + p * 16) + sub16
                qbias[owner, p, half, 2 * s + j] = jnp.where(first > pos, HIDDEN, 0.0).astype(
                    jnp.bfloat16
                )
        return 0

    def turn(b):
        block = vbuf[b].reshape(512, HD).astype(jnp.float32)
        vt[:HD, b * 512 : (b + 1) * 512] = jnp.transpose(block).astype(jnp.bfloat16)

    vt[HD:, :] = jnp.ones((16, KEYS), jnp.bfloat16)
    turn(0)

    def forward(d, p):
        for w in range(2):
            hop[d - 1, p, w].wait_recv()
            way = 1 - 2 * w
            hop[d, p, w] = q_send(4 * (d - 1) + 2 * p + w, -way * (d - 1) % NY, way, p)

    k_right.wait_recv()
    k_far = kv_send(4, kbuf, 3, 1)
    v_left.wait_recv()
    v_far = kv_send(5, vbuf, 1, -1)
    forward(2, 0)
    forward(2, 1)
    lax.fori_loop(0, NY * 8, query_marks, 0)
    turn(1)
    v_right.wait_recv()
    turn(3)
    k_left.wait_recv()
    forward(3, 0)
    forward(3, 1)
    k_far.wait_recv()
    for copy in across:
        copy.wait_recv()

    def unit(u):
        p = u % 2
        group = (u + 2) // 4
        short = (u + 2) % 4 // 2
        return ((2 * p - 1) * (1 - 2 * short) * (4 - group) + NY) % NY, p

    def scores(u, score, peak_ref):
        owner, p = unit(u)
        qa = jnp.concatenate(
            [qbuf[owner, p].reshape(ROWS, HD), qbias[owner, p].reshape(ROWS, HD)], axis=1
        )
        peak = None
        for b in range(NX):
            cut = slice(b * 512, (b + 1) * 512)
            ka = jnp.concatenate([kbuf[b].reshape(512, HD), konehot[cut, :]], axis=1)
            s = lax.dot_general(
                ka, qa, (((1,), (1,)), ((), ())), preferred_element_type=jnp.float32
            )
            score[cut, :] = s
            tile = jnp.max(s.reshape(64, 8, ROWS), axis=0)
            peak = tile if peak is None else jnp.maximum(peak, tile)
            if b == NX - 1:
                peak_ref[...] = jnp.broadcast_to(jnp.max(peak, axis=0, keepdims=True), (8, ROWS))
            yield

    def weigh(u, score, peak_ref):
        owner, p = unit(u)
        peak = peak_ref[0:1, :]
        total = None
        for b in range(NX):
            cut = slice(b * 512, (b + 1) * 512)
            w = jnp.exp2((score[cut, :] - peak) * SCALE).astype(jnp.bfloat16)
            t = jnp.dot(vt[:, cut], w, preferred_element_type=jnp.float32)
            total = t if total is None else total + t
            if b == NX - 1:
                weight = total[HD : HD + 1, :]
                part_o[owner, p] = total[:HD, :] / weight
                part_l[owner, p] = jnp.broadcast_to(
                    jnp.log2(weight) + peak * SCALE, (8, ROWS)
                )
            yield

    def beside(*streams):
        for _ in range(NX):
            for stream in streams:
                next(stream)

    a, b = (score_a, peak_a), (score_b, peak_b)

    def pair(u, more):
        beside(scores(u + 1, *b), weigh(u, *a))
        if more:
            beside(scores(u + 2, *a), weigh(u + 1, *b))
        else:
            beside(weigh(u + 1, *b))

    def merge(o, l, slot):
        m = yl_recv[slot][0:1, :]
        top = jnp.maximum(l, m)
        wa, wb = jnp.exp2(l - top), jnp.exp2(m - top)
        total = wa + wb
        o = o * (wa / total) + yo_recv[slot].astype(jnp.float32) * (wb / total)
        return o, top + jnp.log2(total)

    def y_send(slot, o, l, dev):
        yo_send[slot] = o.astype(jnp.bfloat16)
        yl_send[slot] = jnp.broadcast_to(l, (8, ROWS))
        return (
            send(yo_send.at[slot], yo_recv.at[slot], yo_s.at[slot], yo_r.at[slot], dev),
            send(yl_send.at[slot], yl_recv.at[slot], yl_s.at[slot], yl_r.at[slot], dev),
        )

    yhops = {}

    def y_step(j):
        for short in range(2):
            for p in range(2):
                if short and j == 1:
                    continue
                travel = (2 * p - 1) * (1 - 2 * short)
                owner = travel * (5 - j) % NY
                o, l = part_o[owner, p], part_l[owner, p][0:1, :]
                slot = p * 7 + (2 + j if short else j - 1)
                if j > 1 + short:
                    for copy in yhops[slot - 1]:
                        copy.wait_recv()
                    o, l = merge(o, l, slot - 1)
                yhops[slot] = y_send(slot, o, l, y_dev(travel))

    beside(scores(0, *a))
    v_far.wait_recv()
    turn(2)
    pair(0, False)
    y_step(1)
    for p in range(2):
        for w in range(2):
            hop[3, p, w].wait_recv()
    beside(scores(2, *a))
    for j in range(2, 5):

        def two(i, _):
            pair(4 * j - 6 + 2 * i, True)
            return 0

        lax.fori_loop(0, 2, two, 0)
        y_step(j)
    pair(14, False)

    swaps = []
    for p in range(2):
        o, l = part_o[0, p], part_l[0, p][0:1, :]
        for slot in (p * 7 + 6, p * 7 + 3):
            for copy in yhops[slot]:
                copy.wait_recv()
            o, l = merge(o, l, slot)
        o = jnp.transpose(o).astype(jnp.bfloat16)
        att_send[p] = jnp.where(c == 0, o[PIECE:], o[:PIECE])
        swaps.append(send(att_send.at[p], att.at[p, c], at_s.at[p], at_r.at[p], sibling))
        att[p, c] = jnp.where(c == 0, o[:PIECE], o[PIECE:])

    load_w.wait()

    def project(p):
        rows = jnp.concatenate([att[p, 0], att[p, 1]], axis=1)

        def columns(n, _):
            cut = pl.ds(pl.multiple_of(n * 768, 768), 768)
            r = jnp.dot(rows, wbuf[:, cut], preferred_element_type=jnp.float32)
            proj[p, :, :, cut] = r.reshape(NZ, 16, 768)
            return 0

        lax.fori_loop(0, D // 768, columns, 0)

    zhops = {}
    for j in range(1, 5):
        for short in range(2):
            for p in range(2):
                if short and j == 1:
                    continue
                if j == 1:
                    swaps[p].wait_recv()
                    project(p)
                travel = (2 * p - 1) * (1 - 2 * short)
                r = proj[p, ring(z, travel * (5 - j), NZ)]
                slot = p * 7 + (2 + j if short else j - 1)
                if j > 1 + short:
                    zhops[slot - 1].wait_recv()
                    r = r + z_recv[slot - 1].astype(jnp.float32)
                z_send[slot] = r.astype(jnp.bfloat16)
                zhops[slot] = send(
                    z_send.at[slot], z_recv.at[slot], z_s.at[slot], z_r.at[slot], z_dev(travel)
                )
    for p in range(2):
        r = proj[p, z]
        for slot in (p * 7 + 6, p * 7 + 3):
            zhops[slot].wait_recv()
            r = r + z_recv[slot].astype(jnp.float32)
        out[p * 16 : (p + 1) * 16, :] = r.astype(jnp.bfloat16)
    for copy in sent:
        copy.wait_send()


def body(queries, keys, values, group_lens, dispatch, out_weight):
    bf, f32 = jnp.bfloat16, jnp.float32
    dma = pltpu.SemaphoreType.DMA
    anywhere = pl.BlockSpec(memory_space=pl.ANY)
    smem = pl.BlockSpec(memory_space=pltpu.SMEM)
    return pl.pallas_call(
        kernel,
        out_shape=jax.ShapeDtypeStruct((ROWS // NZ, D), bf),
        in_specs=[smem, smem, anywhere, anywhere, anywhere, anywhere],
        out_specs=pl.BlockSpec(memory_space=pltpu.VMEM),
        scratch_shapes=[
            pltpu.VMEM((NY, 2, 2, NZ, 16, HD), bf),
            pltpu.VMEM((NY, 2, 2, NZ, 16, HD), bf),
            pltpu.VMEM((NX, 2, ROWS, HD), bf),
            pltpu.VMEM((NX, 2, ROWS, HD), bf),
            pltpu.VMEM((HD + 16, KEYS), bf),
            pltpu.VMEM((KEYS, HD), bf),
            pltpu.VMEM((KEYS, ROWS), f32),
            pltpu.VMEM((KEYS, ROWS), f32),
            pltpu.VMEM((8, ROWS), f32),
            pltpu.VMEM((8, ROWS), f32),
            pltpu.VMEM((NY, 2, HD, ROWS), f32),
            pltpu.VMEM((NY, 2, 8, ROWS), f32),
            pltpu.VMEM((14, HD, ROWS), bf),
            pltpu.VMEM((14, 8, ROWS), f32),
            pltpu.VMEM((14, HD, ROWS), bf),
            pltpu.VMEM((14, 8, ROWS), f32),
            pltpu.VMEM((2, 2, PIECE, HD), bf),
            pltpu.VMEM((2, PIECE, HD), bf),
            pltpu.VMEM((2 * HD, D), bf),
            pltpu.VMEM((2, NZ, 16, D), f32),
            pltpu.VMEM((14, 16, D), bf),
            pltpu.VMEM((14, 16, D), bf),
            dma((5,)), dma((4,)), dma((4,)), dma((14,)), dma((14,)), dma((6,)), dma((6,)),
            dma((14,)), dma((14,)), dma((14,)), dma((14,)), dma((2,)), dma((2,)),
            dma((14,)), dma((14,)),
        ],
        compiler_params=pltpu.CompilerParams(
            collective_id=0, has_side_effects=True, vmem_limit_bytes=60 * 1024 * 1024
        ),
        cost_estimate=pl.CostEstimate(
            flops=9_000_000_000, bytes_accessed=6_000_000, transcendentals=8_400_000
        ),
    )(
        group_lens,
        dispatch,
        queries.reshape(NZ, 2, 16, 2 * HD),
        keys,
        values,
        out_weight,
    )


def solution(mesh):
    return jax.shard_map(
        body,
        mesh=mesh,
        in_specs=(P("ctx", "head"), P("ctx", "head"), P("ctx", "head"), P(), P(), P("head", None)),
        out_specs=P(("ctx", "head"), None),
        check_vma=False,
    )
```

```python
import functools

import jax
import jax.numpy as jnp
from jax import lax
from jax.experimental import pallas as pl
from jax.experimental.pallas import tpu as pltpu
from jax.sharding import PartitionSpec as P

HD = 128
SLICE = 64
NX, NY, NZ = 4, 8, 8
ROWS = 256
PIECE = 128
KEYS = NY * 2 * ROWS
D = 3072
HIDDEN = -1e30
LOG2E = 1.4426950408889634
SCALE = HD**-0.5 * LOG2E
MESH = pl.DeviceIdType.MESH


def kernel(
    lens_in, disp_in, q_in, k_in, v_in, w_in, out,
    lens, disp, qbuf, qbias, kbuf, vbuf, vt, konehot, score_a, score_b, peak_a, peak_b,
    part_o, part_m, part_l, yo_send, yl_send, yo_recv, yl_recv, att, att_send, wbuf, proj, z_send, z_recv,
    loc_sem, sib_s, sib_r, q_s, q_r, kv_s, kv_r, yo_s, yo_r, yl_s, yl_r, at_s, at_r, z_s, z_r,
):
    ctx, z = lax.axis_index("ctx"), lax.axis_index("head")
    c = lax.rem(ctx, 2)
    x = lax.rem(ctx // 2, NX)
    y = ctx // (2 * NX)

    def at(yy, xx, cc, zz):
        return ((yy * NX + xx) * 2 + cc, zz)

    def ring(i, step, size):
        return lax.rem(i + step + size, size)

    sibling = at(y, x, 1 - c, z)

    def y_dev(step, core=c):
        return at(ring(y, step, NY), x, core, z)

    def x_dev(step, core=c):
        return at(y, ring(x, step, NX), core, z)

    def z_dev(step):
        return at(y, x, c, ring(z, step, NZ))

    partners = [sibling, x_dev(2), z_dev(-1), z_dev(1)]
    partners += [f(s, core) for f in (x_dev, y_dev) for s in (-1, 1) for core in (c, 1 - c)]
    barrier = pltpu.get_barrier_semaphore()
    for dev in partners:
        pl.semaphore_signal(barrier, inc=1, device_id=dev, device_id_type=MESH)

    mine = pl.ds(pl.multiple_of(c * HD, HD), HD)
    other = pl.ds(pl.multiple_of((1 - c) * HD, HD), HD)
    local = [
        pltpu.make_async_copy(q_in.at[:, p, :, mine], qbuf.at[0, p, c], loc_sem.at[p])
        for p in range(2)
    ]
    local.append(pltpu.make_async_copy(k_in.at[:, mine], kbuf.at[0, c], loc_sem.at[2]))
    local.append(pltpu.make_async_copy(v_in.at[:, mine], vbuf.at[0, c], loc_sem.at[3]))
    local.append(pltpu.make_async_copy(lens_in, lens, loc_sem.at[4]))
    local.append(pltpu.make_async_copy(disp_in, disp, loc_sem.at[5]))
    load_w = pltpu.make_async_copy(w_in, wbuf, loc_sem.at[6])
    for copy in local:
        copy.start()
    pl.semaphore_wait(barrier, len(partners))

    sent = []

    def drain():
        while sent:
            sent.pop(0).wait_send()

    def send(src, dst, s, r, dev):
        copy = pltpu.make_async_remote_copy(
            src_ref=src, dst_ref=dst, send_sem=s, recv_sem=r, device_id=dev, device_id_type=MESH
        )
        copy.start()
        sent.append(copy)
        return copy

    halves = (c, 1 - c)
    lanes = (mine, other)

    def q_first(p, w):
        way = 1 - 2 * w
        return [
            send(
                q_in.at[:, p, :, lanes[t]], qbuf.at[-way % NX, p, c],
                q_s.at[4 * p + 2 * w + t], q_r.at[4 * p + 2 * w + t], x_dev(way, halves[t]),
            )
            for t in range(2)
        ]

    sources, blocks = (k_in, v_in), (kbuf, vbuf)
    hop = {}

    def kv_first(kind):
        for t in range(2):
            for w in range(2):
                way = 1 - 2 * w
                slot = 4 * kind + 2 * w + t
                hop[1, kind, w, t] = send(
                    sources[kind].at[:, lanes[t]], blocks[kind].at[-way % NY, c],
                    kv_s.at[slot], kv_r.at[slot], y_dev(way, halves[t]),
                )

    kv_first(0)
    q_hop = {(p, w): q_first(p, w) for p in range(2) for w in range(2)}
    swaps = [
        send(k_in.at[:, other], kbuf.at[0, c], sib_s.at[2], sib_r.at[2], sibling),
        send(v_in.at[:, other], vbuf.at[0, c], sib_s.at[3], sib_r.at[3], sibling),
    ] + [
        send(q_in.at[:, p, :, other], qbuf.at[0, p, c], sib_s.at[p], sib_r.at[p], sibling)
        for p in range(2)
    ]
    kv_first(1)

    def arrive(d, kind, w, t):
        hop[d, kind, w, t].wait_recv()
        if d == 4 or (d == 3 and kind != w):
            return
        way = 1 - 2 * w
        here, there = -way * d % NY, -way * (d + 1) % NY
        slot = 8 * d + 4 * kind + 2 * w + t if d < 3 else 24 + 2 * kind + t
        ref = blocks[kind]
        hop[d + 1, kind, w, t] = send(
            ref.at[here, halves[t]], ref.at[there, halves[t]],
            kv_s.at[slot], kv_r.at[slot], y_dev(way),
        )

    def arrivals(d):
        if d == 4:
            return [(d, kind, kind, t) for kind in range(2) for t in range(2)]
        return [(d, kind, w, t) for kind in range(2) for t in range(2) for w in range(2)]

    load_w.start()

    for copy in local:
        copy.wait()
    lane = lax.broadcasted_iota(jnp.int32, (1, HD), 1)

    def bounds(g, carry):
        total, first, last = carry
        after = total + lens[g]
        return after, jnp.where(lane == g, total, first), jnp.where(lane == g, after, last)

    _, first, last = lax.fori_loop(
        0, 32, bounds,
        (jnp.int32(0), jnp.full((1, HD), -1, jnp.int32), jnp.zeros((1, HD), jnp.int32)),
    )
    sub64 = lax.broadcasted_iota(jnp.int32, (SLICE, HD), 0)
    sub16 = lax.broadcasted_iota(jnp.int32, (16, HD), 0)

    def key_marks(s, _):
        block = ring(y, s // 8, NY)
        pos = disp[(block * NX + x) * 8 + lax.rem(s, 8)] * SLICE + sub64
        inside = jnp.where((first <= pos) & (pos < last), 1.0, 0.0)
        konehot[pl.ds(pl.multiple_of(s * SLICE, SLICE), SLICE), :] = inside.astype(jnp.bfloat16)
        return 0

    lax.fori_loop(0, KEYS // SLICE, key_marks, 0)

    def query_marks(i, _):
        owner, half, s = i // 8, lax.rem(i // 4, 2), lax.rem(i, 4)
        start = disp[(y * NX + ring(x, owner, NX)) * 8 + half * 4 + s] * SLICE
        for j in range(2):
            for p in range(2):
                pos = start + (j * 32 + p * 16) + sub16
                qbias[owner, p, half, 2 * s + j] = jnp.where(first > pos, HIDDEN, 0.0).astype(
                    jnp.bfloat16
                )
        return 0

    def turn(b):
        block = vbuf[b].reshape(512, HD).astype(jnp.float32)
        vt[:HD, b * 512 : (b + 1) * 512] = jnp.transpose(block).astype(jnp.bfloat16)

    vt[HD:, :] = jnp.ones((16, KEYS), jnp.bfloat16)

    lax.fori_loop(0, NX * 8, query_marks, 0)
    for copy in swaps:
        copy.wait_recv()
    turn(0)

    def level_blocks(d):
        return (d,) if d in (0, 4) else (d, NY - d)

    def scores(d, owner, p, score, peak_ref):
        qa = jnp.concatenate(
            [qbuf[owner, p].reshape(ROWS, HD), qbias[owner, p].reshape(ROWS, HD)], axis=1
        )
        peak = None
        for i, b in enumerate(level_blocks(d)):
            ka = jnp.concatenate(
                [kbuf[b].reshape(512, HD), konehot[b * 512 : (b + 1) * 512, :]], axis=1
            )
            s = lax.dot_general(
                ka, qa, (((1,), (1,)), ((), ())), preferred_element_type=jnp.float32
            )
            score[i * 512 : (i + 1) * 512, :] = s
            tile = jnp.max(s.reshape(64, 8, ROWS), axis=0)
            peak = tile if peak is None else jnp.maximum(peak, tile)
            if b == level_blocks(d)[-1]:
                peak_ref[...] = jnp.broadcast_to(jnp.max(peak, axis=0, keepdims=True), (8, ROWS))
            yield

    def weigh(d, owner, p, score, peak_ref):
        peak = peak_ref[0:1, :]
        if d > 0:
            before = part_m[owner, p][0:1, :]
            peak = jnp.maximum(before, peak)
        total = None
        for i, b in enumerate(level_blocks(d)):
            w = jnp.exp2((score[i * 512 : (i + 1) * 512, :] - peak) * SCALE).astype(jnp.bfloat16)
            t = jnp.dot(
                vt[:, b * 512 : (b + 1) * 512], w, preferred_element_type=jnp.float32
            )
            total = t if total is None else total + t
            if b == level_blocks(d)[-1]:
                o, l = total[:HD, :], total[HD : HD + 1, :]
                if d > 0:
                    factor = jnp.exp2((before - peak) * SCALE)
                    o = part_o[owner, p] * factor + o
                    l = part_l[owner, p][0:1, :] * factor + l
                if d < 4 or owner == 0:
                    part_o[owner, p] = o
                    part_m[owner, p] = jnp.broadcast_to(peak, (8, ROWS))
                    part_l[owner, p] = jnp.broadcast_to(l, (8, ROWS))
                else:
                    give(owner, p, o, peak, l)
            yield

    def beside(*streams):
        live = list(streams)
        while live:
            live = [stream for stream in live if next(stream, True) is None]

    sub8 = lax.broadcasted_iota(jnp.int32, (8, ROWS), 0)
    given = {}

    def give(owner, p, o, peak, l):
        slot = 3 * p + owner - 1
        yo_send[slot] = o.astype(jnp.bfloat16)
        yl_send[slot] = jnp.where(sub8 < 4, peak, l)
        dev = x_dev(owner)
        given[slot] = (
            send(yo_send.at[slot], yo_recv.at[slot], yo_s.at[slot], yo_r.at[slot], dev),
            send(yl_send.at[slot], yl_recv.at[slot], yl_s.at[slot], yl_r.at[slot], dev),
        )

    buffers = ((score_a, peak_a), (score_b, peak_b))

    def stage(d, units, tasks):
        beside(scores(d, *units[0], *buffers[0]))
        for i, unit in enumerate(units):
            for task in tasks[i : i + 1]:
                arrive(*task)
            streams = [weigh(d, *unit, *buffers[i % 2])]
            if i + 1 < len(units):
                streams.insert(0, scores(d, *units[i + 1], *buffers[(i + 1) % 2]))
            beside(*streams)
        for task in tasks[len(units) :]:
            arrive(*task)

    order = [(owner, p) for owner in (2, 1, 3, 0) for p in range(2)]
    stage(0, order[6:], [])
    q_far = []
    for t in range(2):
        for p in range(2):
            q_hop[p, p][t].wait_recv()
            way = 1 - 2 * p
            slot = 8 + 2 * p + t
            q_far.append(
                send(
                    qbuf.at[-way % NX, p, halves[t]], qbuf.at[2, p, halves[t]],
                    q_s.at[slot], q_r.at[slot], x_dev(way),
                )
            )
    for task in arrivals(1)[:2]:
        arrive(*task)
    for p in range(2):
        for copy in q_hop[p, 1 - p]:
            copy.wait_recv()
    stage(0, order[2:6], arrivals(1)[2:])
    for copy in q_far:
        copy.wait_recv()
    stage(0, order[:2], [])
    for d in range(1, 4):
        if d == 3:
            drain()
        turn(d)
        turn(NY - d)
        stage(d, order, arrivals(d + 1))
    turn(4)
    stage(4, order, [])

    swaps = []
    for p in range(2):
        slots = [3 * p + k for k in range(3)]
        for slot in slots:
            for copy in given[slot]:
                copy.wait_recv()
        tops = [part_m[0, p][0:1, :]] + [yl_recv[slot][0:1, :] for slot in slots]
        sums = [part_l[0, p][0:1, :]] + [yl_recv[slot][4:5, :] for slot in slots]
        top = functools.reduce(jnp.maximum, tops)
        factors = [jnp.exp2((m - top) * SCALE) for m in tops]
        inverse = 1.0 / sum(f * l for f, l in zip(factors, sums))
        o = part_o[0, p] * (factors[0] * inverse)
        for f, slot in zip(factors[1:], slots):
            o = o + yo_recv[slot].astype(jnp.float32) * (f * inverse)
        o = jnp.transpose(o).astype(jnp.bfloat16)
        att_send[p] = jnp.where(c == 0, o[PIECE:], o[:PIECE])
        swaps.append(send(att_send.at[p], att.at[p, c], at_s.at[p], at_r.at[p], sibling))
        att[p, c] = jnp.where(c == 0, o[:PIECE], o[PIECE:])

    load_w.wait()

    def project(p):
        rows = jnp.concatenate([att[p, 0], att[p, 1]], axis=1)

        def columns(n, _):
            cut = pl.ds(pl.multiple_of(n * 768, 768), 768)
            r = jnp.dot(rows, wbuf[:, cut], preferred_element_type=jnp.float32)
            proj[p, :, :, cut] = r.reshape(NZ, 16, 768)
            return 0

        lax.fori_loop(0, D // 768, columns, 0)

    zhops = {}
    half = D // 2
    for j in range(1, 5):
        if j == 3:
            drain()
        for short in range(2):
            for p in range(2):
                if short and j == 4:
                    continue
                if j == 1 and not short:
                    swaps[p].wait_recv()
                    project(p)
                for h in range(2):
                    travel = (2 * p - 1) * (1 - 2 * short) * (1 - 2 * h)
                    owner = ring(z, travel * (5 - j - short), NZ)
                    r = proj[p, owner, :, h * half : (h + 1) * half]
                    slot = (2 * p + h) * 7 + 4 * short + j - 1
                    if j > 1:
                        zhops[slot - 1].wait_recv()
                        r = r + z_recv[slot - 1].astype(jnp.float32)
                    z_send[slot] = r.astype(jnp.bfloat16)
                    zhops[slot] = send(
                        z_send.at[slot], z_recv.at[slot], z_s.at[slot], z_r.at[slot], z_dev(travel)
                    )
    for p in range(2):
        for h in range(2):
            r = proj[p, z, :, h * half : (h + 1) * half]
            for slot in ((2 * p + h) * 7 + 6, (2 * p + h) * 7 + 3):
                zhops[slot].wait_recv()
                r = r + z_recv[slot].astype(jnp.float32)
            out[p * 16 : (p + 1) * 16, h * half : (h + 1) * half] = r.astype(jnp.bfloat16)
    drain()


def body(queries, keys, values, group_lens, dispatch, out_weight):
    bf, f32 = jnp.bfloat16, jnp.float32
    dma = pltpu.SemaphoreType.DMA
    anywhere = pl.BlockSpec(memory_space=pl.ANY)
    return pl.pallas_call(
        kernel,
        out_shape=jax.ShapeDtypeStruct((ROWS // NZ, D), bf),
        in_specs=[anywhere] * 6,
        out_specs=pl.BlockSpec(memory_space=pltpu.VMEM),
        scratch_shapes=[
            pltpu.SMEM((32,), jnp.int32),
            pltpu.SMEM((256,), jnp.int32),
            pltpu.VMEM((NX, 2, 2, NZ, 16, HD), bf),
            pltpu.VMEM((NX, 2, 2, NZ, 16, HD), bf),
            pltpu.VMEM((NY, 2, ROWS, HD), bf),
            pltpu.VMEM((NY, 2, ROWS, HD), bf),
            pltpu.VMEM((HD + 16, KEYS), bf),
            pltpu.VMEM((KEYS, HD), bf),
            pltpu.VMEM((1024, ROWS), f32),
            pltpu.VMEM((1024, ROWS), f32),
            pltpu.VMEM((8, ROWS), f32),
            pltpu.VMEM((8, ROWS), f32),
            pltpu.VMEM((NX, 2, HD, ROWS), f32),
            pltpu.VMEM((NX, 2, 8, ROWS), f32),
            pltpu.VMEM((NX, 2, 8, ROWS), f32),
            pltpu.VMEM((6, HD, ROWS), bf),
            pltpu.VMEM((6, 8, ROWS), f32),
            pltpu.VMEM((6, HD, ROWS), bf),
            pltpu.VMEM((6, 8, ROWS), f32),
            pltpu.VMEM((2, 2, PIECE, HD), bf),
            pltpu.VMEM((2, PIECE, HD), bf),
            pltpu.VMEM((2 * HD, D), bf),
            pltpu.VMEM((2, NZ, 16, D), f32),
            pltpu.VMEM((28, 16, D // 2), bf),
            pltpu.VMEM((28, 16, D // 2), bf),
            dma((7,)), dma((4,)), dma((4,)), dma((12,)), dma((12,)), dma((28,)), dma((28,)),
            dma((6,)), dma((6,)), dma((6,)), dma((6,)), dma((2,)), dma((2,)),
            dma((28,)), dma((28,)),
        ],
        compiler_params=pltpu.CompilerParams(
            collective_id=0, has_side_effects=True, vmem_limit_bytes=60 * 1024 * 1024
        ),
        cost_estimate=pl.CostEstimate(
            flops=9_000_000_000, bytes_accessed=6_000_000, transcendentals=8_400_000
        ),
    )(
        group_lens,
        dispatch,
        queries.reshape(NZ, 2, 16, 2 * HD),
        keys,
        values,
        out_weight,
    )


def solution(mesh):
    return jax.shard_map(
        body,
        mesh=mesh,
        in_specs=(P("ctx", "head"), P("ctx", "head"), P("ctx", "head"), P(), P(), P("head", None)),
        out_specs=P(("ctx", "head"), None),
        check_vma=False,
    )
```

```python
import functools

import jax
import jax.numpy as jnp
from jax import lax
from jax.experimental import pallas as pl
from jax.experimental.pallas import tpu as pltpu
from jax.sharding import PartitionSpec as P

HD = 128
SLICE = 64
NX, NY, NZ = 4, 8, 8
ROWS = 256
PIECE = 128
KEYS = NY * 2 * ROWS
D = 3072
HIDDEN = -1e30
LOG2E = 1.4426950408889634
SCALE = HD**-0.5 * LOG2E
MESH = pl.DeviceIdType.MESH


def kernel(
    lens_in, disp_in, q_in, k_in, v_in, w_in, out,
    lens, disp, qbuf, qbias, kbuf, vbuf, vt, konehot, score_a, score_b, peak_a, peak_b,
    part_o, part_m, part_l, yo_send, yl_send, yo_recv, yl_recv, att, att_send, wbuf, proj, z_send, z_recv,
    loc_sem, sib_s, sib_r, q_s, q_r, kv_s, kv_r, yo_s, yo_r, yl_s, yl_r, at_s, at_r, z_s, z_r,
):
    ctx, z = lax.axis_index("ctx"), lax.axis_index("head")
    c = lax.rem(ctx, 2)
    x = lax.rem(ctx // 2, NX)
    y = ctx // (2 * NX)

    def at(yy, xx, cc, zz):
        return ((yy * NX + xx) * 2 + cc, zz)

    def ring(i, step, size):
        return lax.rem(i + step + size, size)

    sibling = at(y, x, 1 - c, z)

    def y_dev(step, core=c):
        return at(ring(y, step, NY), x, core, z)

    def x_dev(step, core=c):
        return at(y, ring(x, step, NX), core, z)

    def z_dev(step):
        return at(y, x, c, ring(z, step, NZ))

    partners = [sibling, x_dev(2), z_dev(-1), z_dev(1)]
    partners += [f(s, core) for f in (x_dev, y_dev) for s in (-1, 1) for core in (c, 1 - c)]
    barrier = pltpu.get_barrier_semaphore()
    for dev in partners:
        pl.semaphore_signal(barrier, inc=1, device_id=dev, device_id_type=MESH)

    mine = pl.ds(pl.multiple_of(c * HD, HD), HD)
    other = pl.ds(pl.multiple_of((1 - c) * HD, HD), HD)
    local = [
        pltpu.make_async_copy(q_in.at[:, p, :, mine], qbuf.at[0, p, c], loc_sem.at[p])
        for p in range(2)
    ]
    local.append(pltpu.make_async_copy(k_in.at[:, mine], kbuf.at[0, c], loc_sem.at[2]))
    local.append(pltpu.make_async_copy(v_in.at[:, mine], vbuf.at[0, c], loc_sem.at[3]))
    local.append(pltpu.make_async_copy(lens_in, lens, loc_sem.at[4]))
    local.append(pltpu.make_async_copy(disp_in, disp, loc_sem.at[5]))
    load_w = pltpu.make_async_copy(w_in, wbuf, loc_sem.at[6])
    for copy in local:
        copy.start()
    pl.semaphore_wait(barrier, len(partners))

    sent = []

    def drain():
        while sent:
            sent.pop(0).wait_send()

    def send(src, dst, s, r, dev):
        copy = pltpu.make_async_remote_copy(
            src_ref=src, dst_ref=dst, send_sem=s, recv_sem=r, device_id=dev, device_id_type=MESH
        )
        copy.start()
        sent.append(copy)
        return copy

    halves = (c, 1 - c)
    lanes = (mine, other)

    def q_first(p, w):
        way = 1 - 2 * w
        return [
            send(
                q_in.at[:, p, :, lanes[t]], qbuf.at[-way % NX, p, c],
                q_s.at[4 * p + 2 * w + t], q_r.at[4 * p + 2 * w + t], x_dev(way, halves[t]),
            )
            for t in range(2)
        ]

    sources, blocks = (k_in, v_in), (kbuf, vbuf)
    hop = {}

    def kv_first(kind):
        for t in range(2):
            for w in range(2):
                way = 1 - 2 * w
                slot = 4 * kind + 2 * w + t
                hop[1, kind, w, t] = send(
                    sources[kind].at[:, lanes[t]], blocks[kind].at[-way % NY, c],
                    kv_s.at[slot], kv_r.at[slot], y_dev(way, halves[t]),
                )

    kv_first(0)
    q_hop = {(p, w): q_first(p, w) for p in range(2) for w in range(2)}
    swaps = [
        send(k_in.at[:, other], kbuf.at[0, c], sib_s.at[2], sib_r.at[2], sibling),
        send(v_in.at[:, other], vbuf.at[0, c], sib_s.at[3], sib_r.at[3], sibling),
    ] + [
        send(q_in.at[:, p, :, other], qbuf.at[0, p, c], sib_s.at[p], sib_r.at[p], sibling)
        for p in range(2)
    ]
    kv_first(1)

    def arrive(d, kind, w, t):
        hop[d, kind, w, t].wait_recv()
        if d == 4 or (d == 3 and kind != w):
            return
        way = 1 - 2 * w
        here, there = -way * d % NY, -way * (d + 1) % NY
        slot = 8 * d + 4 * kind + 2 * w + t if d < 3 else 24 + 2 * kind + t
        ref = blocks[kind]
        hop[d + 1, kind, w, t] = send(
            ref.at[here, halves[t]], ref.at[there, halves[t]],
            kv_s.at[slot], kv_r.at[slot], y_dev(way),
        )

    def arrivals(d):
        if d == 4:
            return [(d, kind, kind, t) for kind in range(2) for t in range(2)]
        return [(d, kind, w, t) for kind in range(2) for t in range(2) for w in range(2)]

    load_w.start()

    for copy in local:
        copy.wait()
    lane = lax.broadcasted_iota(jnp.int32, (1, HD), 1)

    def bounds(g, carry):
        total, first, last = carry
        after = total + lens[g]
        return after, jnp.where(lane == g, total, first), jnp.where(lane == g, after, last)

    _, first, last = lax.fori_loop(
        0, 32, bounds,
        (jnp.int32(0), jnp.full((1, HD), -1, jnp.int32), jnp.zeros((1, HD), jnp.int32)),
    )
    sub64 = lax.broadcasted_iota(jnp.int32, (SLICE, HD), 0)
    sub16 = lax.broadcasted_iota(jnp.int32, (16, HD), 0)

    def key_marks(s, _):
        block = ring(y, s // 8, NY)
        pos = disp[(block * NX + x) * 8 + lax.rem(s, 8)] * SLICE + sub64
        inside = jnp.where((first <= pos) & (pos < last), 1.0, 0.0)
        konehot[pl.ds(pl.multiple_of(s * SLICE, SLICE), SLICE), :] = inside.astype(jnp.bfloat16)
        return 0

    def mark(b):
        lax.fori_loop(8 * b, 8 * b + 8, key_marks, 0)

    def query_marks(i, _):
        owner, half, s = i // 8, lax.rem(i // 4, 2), lax.rem(i, 4)
        start = disp[(y * NX + ring(x, owner, NX)) * 8 + half * 4 + s] * SLICE
        for j in range(2):
            for p in range(2):
                pos = start + (j * 32 + p * 16) + sub16
                qbias[owner, p, half, 2 * s + j] = jnp.where(first > pos, HIDDEN, 0.0).astype(
                    jnp.bfloat16
                )
        return 0

    def turn(b):
        block = vbuf[b].reshape(512, HD).astype(jnp.float32)
        vt[:HD, b * 512 : (b + 1) * 512] = jnp.transpose(block).astype(jnp.bfloat16)

    vt[HD:, :] = jnp.ones((16, KEYS), jnp.bfloat16)

    lax.fori_loop(0, NX * 8, query_marks, 0)
    mark(0)
    for copy in swaps:
        copy.wait_recv()
    turn(0)

    def level_blocks(d):
        return (d,) if d in (0, 4) else (d, NY - d)

    def scores(d, owner, p, score, peak_ref):
        qa = jnp.concatenate(
            [qbuf[owner, p].reshape(ROWS, HD), qbias[owner, p].reshape(ROWS, HD)], axis=1
        )
        peak = None
        for i, b in enumerate(level_blocks(d)):
            ka = jnp.concatenate(
                [kbuf[b].reshape(512, HD), konehot[b * 512 : (b + 1) * 512, :]], axis=1
            )
            s = lax.dot_general(
                ka, qa, (((1,), (1,)), ((), ())), preferred_element_type=jnp.float32
            )
            score[i * 512 : (i + 1) * 512, :] = s
            tile = jnp.max(s.reshape(64, 8, ROWS), axis=0)
            peak = tile if peak is None else jnp.maximum(peak, tile)
            if b == level_blocks(d)[-1]:
                peak_ref[...] = jnp.broadcast_to(jnp.max(peak, axis=0, keepdims=True), (8, ROWS))
            yield

    def weigh(d, owner, p, score, peak_ref):
        peak = peak_ref[0:1, :]
        if d > 0:
            before = part_m[owner, p][0:1, :]
            peak = jnp.maximum(before, peak)
        total = None
        for i, b in enumerate(level_blocks(d)):
            w = jnp.exp2((score[i * 512 : (i + 1) * 512, :] - peak) * SCALE).astype(jnp.bfloat16)
            t = jnp.dot(
                vt[:, b * 512 : (b + 1) * 512], w, preferred_element_type=jnp.float32
            )
            total = t if total is None else total + t
            if b == level_blocks(d)[-1]:
                o, l = total[:HD, :], total[HD : HD + 1, :]
                if d > 0:
                    factor = jnp.exp2((before - peak) * SCALE)
                    o = part_o[owner, p] * factor + o
                    l = part_l[owner, p][0:1, :] * factor + l
                if d < 4 or owner == 0:
                    part_o[owner, p] = o
                    part_m[owner, p] = jnp.broadcast_to(peak, (8, ROWS))
                    part_l[owner, p] = jnp.broadcast_to(l, (8, ROWS))
                else:
                    give(owner, p, o, peak, l)
            yield

    def beside(*streams):
        live = list(streams)
        while live:
            live = [stream for stream in live if next(stream, True) is None]

    sub8 = lax.broadcasted_iota(jnp.int32, (8, ROWS), 0)
    given = {}

    def give(owner, p, o, peak, l):
        slot = 3 * p + owner - 1
        yo_send[slot] = o.astype(jnp.bfloat16)
        yl_send[slot] = jnp.where(sub8 < 4, peak, l)
        dev = x_dev(owner)
        given[slot] = (
            send(yo_send.at[slot], yo_recv.at[slot], yo_s.at[slot], yo_r.at[slot], dev),
            send(yl_send.at[slot], yl_recv.at[slot], yl_s.at[slot], yl_r.at[slot], dev),
        )

    buffers = ((score_a, peak_a), (score_b, peak_b))

    def stage(d, units, tasks, marks=(), ready=None):
        beside(scores(d, *units[0], *buffers[0]))
        if ready is not None:
            ready()
        for i, unit in enumerate(units):
            for task in tasks[i : i + 1]:
                arrive(*task)
            if i < len(marks):
                mark(marks[i])
            streams = [weigh(d, *unit, *buffers[i % 2])]
            if i + 1 < len(units):
                streams.insert(0, scores(d, *units[i + 1], *buffers[(i + 1) % 2]))
            beside(*streams)
        for task in tasks[len(units) :]:
            arrive(*task)

    order = [(owner, p) for owner in (2, 1, 3, 0) for p in range(2)]
    stage(0, order[6:], [])
    q_far = []
    for t in range(2):
        for p in range(2):
            q_hop[p, p][t].wait_recv()
            way = 1 - 2 * p
            slot = 8 + 2 * p + t
            q_far.append(
                send(
                    qbuf.at[-way % NX, p, halves[t]], qbuf.at[2, p, halves[t]],
                    q_s.at[slot], q_r.at[slot], x_dev(way),
                )
            )
    for task in arrivals(1)[:2]:
        arrive(*task)
    for p in range(2):
        for copy in q_hop[p, 1 - p]:
            copy.wait_recv()
    stage(0, order[2:6], arrivals(1)[2:])
    for copy in q_far:
        copy.wait_recv()
    stage(0, order[:2], [], (1, 7))
    for d in range(1, 3):
        turn(d)
        turn(NY - d)
        stage(d, order, arrivals(d + 1), (d + 1, NY - d - 1))
    turn(3)
    turn(5)
    stage(3, order, [], (4,))
    drain()
    for task in arrivals(4)[:2]:
        arrive(*task)

    def last_values():
        for task in arrivals(4)[2:]:
            arrive(*task)
        turn(4)

    stage(4, order[0::2][:3] + order[1::2][:3] + order[6:], [], ready=last_values)

    def finish(p):
        slots = [3 * p + k for k in range(3)]
        for slot in slots:
            for copy in given[slot]:
                copy.wait_recv()
        tops = [part_m[0, p][0:1, :]] + [yl_recv[slot][0:1, :] for slot in slots]
        sums = [part_l[0, p][0:1, :]] + [yl_recv[slot][4:5, :] for slot in slots]
        top = functools.reduce(jnp.maximum, tops)
        factors = [jnp.exp2((m - top) * SCALE) for m in tops]
        inverse = 1.0 / sum(f * l for f, l in zip(factors, sums))
        o = part_o[0, p] * (factors[0] * inverse)
        for f, slot in zip(factors[1:], slots):
            o = o + yo_recv[slot].astype(jnp.float32) * (f * inverse)
        o = jnp.transpose(o).astype(jnp.bfloat16)
        att_send[p] = jnp.where(c == 0, o[PIECE:], o[:PIECE])
        back = send(att_send.at[p], att.at[p, c], at_s.at[p], at_r.at[p], sibling)
        att[p, c] = jnp.where(c == 0, o[:PIECE], o[PIECE:])
        back.wait_recv()

    def project(p):
        rows = jnp.concatenate([att[p, 0], att[p, 1]], axis=1)

        def columns(n, _):
            cut = pl.ds(pl.multiple_of(n * 768, 768), 768)
            r = jnp.dot(rows, wbuf[:, cut], preferred_element_type=jnp.float32)
            proj[p, :, :, cut] = r.reshape(NZ, 16, 768)
            return 0

        lax.fori_loop(0, D // 768, columns, 0)

    zhops = {}
    half = D // 2

    def z_step(j, p):
        for short in range(2):
            if short and j == 4:
                continue
            for h in range(2):
                travel = (2 * p - 1) * (1 - 2 * short) * (1 - 2 * h)
                owner = ring(z, travel * (5 - j - short), NZ)
                r = proj[p, owner, :, h * half : (h + 1) * half]
                slot = (2 * p + h) * 7 + 4 * short + j - 1
                if j > 1:
                    zhops[slot - 1].wait_recv()
                    r = r + z_recv[slot - 1].astype(jnp.float32)
                z_send[slot] = r.astype(jnp.bfloat16)
                zhops[slot] = send(
                    z_send.at[slot], z_recv.at[slot], z_s.at[slot], z_r.at[slot], z_dev(travel)
                )

    load_w.wait()
    for p in range(2):
        finish(p)
        project(p)
        z_step(1, p)
    for j in range(2, 5):
        if j == 3:
            drain()
        for p in range(2):
            z_step(j, p)
    for p in range(2):
        for h in range(2):
            r = proj[p, z, :, h * half : (h + 1) * half]
            for slot in ((2 * p + h) * 7 + 6, (2 * p + h) * 7 + 3):
                zhops[slot].wait_recv()
                r = r + z_recv[slot].astype(jnp.float32)
            out[p * 16 : (p + 1) * 16, h * half : (h + 1) * half] = r.astype(jnp.bfloat16)
    drain()


def body(queries, keys, values, group_lens, dispatch, out_weight):
    bf, f32 = jnp.bfloat16, jnp.float32
    dma = pltpu.SemaphoreType.DMA
    anywhere = pl.BlockSpec(memory_space=pl.ANY)
    return pl.pallas_call(
        kernel,
        out_shape=jax.ShapeDtypeStruct((ROWS // NZ, D), bf),
        in_specs=[anywhere] * 6,
        out_specs=pl.BlockSpec(memory_space=pltpu.VMEM),
        scratch_shapes=[
            pltpu.SMEM((32,), jnp.int32),
            pltpu.SMEM((256,), jnp.int32),
            pltpu.VMEM((NX, 2, 2, NZ, 16, HD), bf),
            pltpu.VMEM((NX, 2, 2, NZ, 16, HD), bf),
            pltpu.VMEM((NY, 2, ROWS, HD), bf),
            pltpu.VMEM((NY, 2, ROWS, HD), bf),
            pltpu.VMEM((HD + 16, KEYS), bf),
            pltpu.VMEM((KEYS, HD), bf),
            pltpu.VMEM((1024, ROWS), f32),
            pltpu.VMEM((1024, ROWS), f32),
            pltpu.VMEM((8, ROWS), f32),
            pltpu.VMEM((8, ROWS), f32),
            pltpu.VMEM((NX, 2, HD, ROWS), f32),
            pltpu.VMEM((NX, 2, 8, ROWS), f32),
            pltpu.VMEM((NX, 2, 8, ROWS), f32),
            pltpu.VMEM((6, HD, ROWS), bf),
            pltpu.VMEM((6, 8, ROWS), f32),
            pltpu.VMEM((6, HD, ROWS), bf),
            pltpu.VMEM((6, 8, ROWS), f32),
            pltpu.VMEM((2, 2, PIECE, HD), bf),
            pltpu.VMEM((2, PIECE, HD), bf),
            pltpu.VMEM((2 * HD, D), bf),
            pltpu.VMEM((2, NZ, 16, D), f32),
            pltpu.VMEM((28, 16, D // 2), bf),
            pltpu.VMEM((28, 16, D // 2), bf),
            dma((7,)), dma((4,)), dma((4,)), dma((12,)), dma((12,)), dma((28,)), dma((28,)),
            dma((6,)), dma((6,)), dma((6,)), dma((6,)), dma((2,)), dma((2,)),
            dma((28,)), dma((28,)),
        ],
        compiler_params=pltpu.CompilerParams(
            collective_id=0, has_side_effects=True, vmem_limit_bytes=60 * 1024 * 1024
        ),
        cost_estimate=pl.CostEstimate(
            flops=9_000_000_000, bytes_accessed=6_000_000, transcendentals=8_400_000
        ),
    )(
        group_lens,
        dispatch,
        queries.reshape(NZ, 2, 16, 2 * HD),
        keys,
        values,
        out_weight,
    )


def solution(mesh):
    return jax.shard_map(
        body,
        mesh=mesh,
        in_specs=(P("ctx", "head"), P("ctx", "head"), P("ctx", "head"), P(), P(), P("head", None)),
        out_specs=P(("ctx", "head"), None),
        check_vma=False,
    )
```

```python
import functools

import jax
import jax.numpy as jnp
from jax import lax
from jax.experimental import pallas as pl
from jax.experimental.pallas import tpu as pltpu
from jax.sharding import PartitionSpec as P

HD = 128
SLICE = 64
NX, NY, NZ = 4, 8, 8
ROWS = 256
PIECE = 128
KEYS = NY * 2 * ROWS
D = 3072
HIDDEN = -1e30
LOG2E = 1.4426950408889634
SCALE = HD**-0.5 * LOG2E
MESH = pl.DeviceIdType.MESH


def kernel(
    lens_in, disp_in, q_in, k_in, v_in, w_in, out,
    lens, disp, qbuf, qbias, kbuf, vbuf, vt, konehot, score_a, score_b, peak_a, peak_b,
    part_o, part_m, part_l, yo_send, yl_send, yo_recv, yl_recv, att, att_send, wbuf, proj, z_send, z_recv,
    loc_sem, sib_s, sib_r, q_s, q_r, kv_s, kv_r, yo_s, yo_r, yl_s, yl_r, at_s, at_r, z_s, z_r,
):
    ctx, z = lax.axis_index("ctx"), lax.axis_index("head")
    c = lax.rem(ctx, 2)
    x = lax.rem(ctx // 2, NX)
    y = ctx // (2 * NX)

    def at(yy, xx, cc, zz):
        return ((yy * NX + xx) * 2 + cc, zz)

    def ring(i, step, size):
        return lax.rem(i + step + size, size)

    sibling = at(y, x, 1 - c, z)

    def y_dev(step, core=c):
        return at(ring(y, step, NY), x, core, z)

    def x_dev(step, core=c):
        return at(y, ring(x, step, NX), core, z)

    def z_dev(step):
        return at(y, x, c, ring(z, step, NZ))

    partners = [sibling, x_dev(2), z_dev(-1), z_dev(1)]
    partners += [f(s, core) for f in (x_dev, y_dev) for s in (-1, 1) for core in (c, 1 - c)]
    barrier = pltpu.get_barrier_semaphore()
    for dev in partners:
        pl.semaphore_signal(barrier, inc=1, device_id=dev, device_id_type=MESH)

    mine = pl.ds(pl.multiple_of(c * HD, HD), HD)
    other = pl.ds(pl.multiple_of((1 - c) * HD, HD), HD)
    local = [
        pltpu.make_async_copy(q_in.at[:, p, :, mine], qbuf.at[0, p, c], loc_sem.at[p])
        for p in range(2)
    ]
    local.append(pltpu.make_async_copy(k_in.at[:, mine], kbuf.at[0, c], loc_sem.at[2]))
    local.append(pltpu.make_async_copy(v_in.at[:, mine], vbuf.at[0, c], loc_sem.at[3]))
    local.append(pltpu.make_async_copy(lens_in, lens, loc_sem.at[4]))
    local.append(pltpu.make_async_copy(disp_in, disp, loc_sem.at[5]))
    load_w = pltpu.make_async_copy(w_in, wbuf, loc_sem.at[6])
    for copy in local:
        copy.start()
    pl.semaphore_wait(barrier, len(partners))

    sent = []

    def drain():
        while sent:
            sent.pop(0).wait_send()

    def send(src, dst, s, r, dev):
        copy = pltpu.make_async_remote_copy(
            src_ref=src, dst_ref=dst, send_sem=s, recv_sem=r, device_id=dev, device_id_type=MESH
        )
        copy.start()
        sent.append(copy)
        return copy

    halves = (c, 1 - c)
    lanes = (mine, other)

    def q_first(p, w):
        way = 1 - 2 * w
        return [
            send(
                q_in.at[:, p, :, lanes[t]], qbuf.at[-way % NX, p, c],
                q_s.at[4 * p + 2 * w + t], q_r.at[4 * p + 2 * w + t], x_dev(way, halves[t]),
            )
            for t in range(2)
        ]

    sources, blocks = (k_in, v_in), (kbuf, vbuf)
    hop = {}

    def kv_first(kind):
        for t in range(2):
            for w in range(2):
                way = 1 - 2 * w
                slot = 4 * kind + 2 * w + t
                hop[1, kind, w, t] = send(
                    sources[kind].at[:, lanes[t]], blocks[kind].at[-way % NY, c],
                    kv_s.at[slot], kv_r.at[slot], y_dev(way, halves[t]),
                )

    kv_first(0)
    q_hop = {(p, w): q_first(p, w) for p in range(2) for w in range(2)}
    swaps = [
        send(k_in.at[:, other], kbuf.at[0, c], sib_s.at[2], sib_r.at[2], sibling),
        send(v_in.at[:, other], vbuf.at[0, c], sib_s.at[3], sib_r.at[3], sibling),
    ] + [
        send(q_in.at[:, p, :, other], qbuf.at[0, p, c], sib_s.at[p], sib_r.at[p], sibling)
        for p in range(2)
    ]
    kv_first(1)

    def arrive(d, kind, w, t):
        hop[d, kind, w, t].wait_recv()
        if d == 4 or (d == 3 and kind != w):
            return
        way = 1 - 2 * w
        here, there = -way * d % NY, -way * (d + 1) % NY
        slot = 8 * d + 4 * kind + 2 * w + t if d < 3 else 24 + 2 * kind + t
        ref = blocks[kind]
        hop[d + 1, kind, w, t] = send(
            ref.at[here, halves[t]], ref.at[there, halves[t]],
            kv_s.at[slot], kv_r.at[slot], y_dev(way),
        )

    def arrivals(d):
        if d == 4:
            return [(d, kind, kind, t) for kind in range(2) for t in range(2)]
        return [(d, kind, w, t) for kind in range(2) for t in range(2) for w in range(2)]

    load_w.start()

    for copy in local:
        copy.wait()
    lane = lax.broadcasted_iota(jnp.int32, (1, HD), 1)

    def bounds(g, carry):
        total, first, last = carry
        after = total + lens[g]
        return after, jnp.where(lane == g, total, first), jnp.where(lane == g, after, last)

    _, first, last = lax.fori_loop(
        0, 32, bounds,
        (jnp.int32(0), jnp.full((1, HD), -1, jnp.int32), jnp.zeros((1, HD), jnp.int32)),
    )
    sub64 = lax.broadcasted_iota(jnp.int32, (SLICE, HD), 0)
    sub16 = lax.broadcasted_iota(jnp.int32, (16, HD), 0)

    def key_marks(s, _):
        block = ring(y, s // 8, NY)
        pos = disp[(block * NX + x) * 8 + lax.rem(s, 8)] * SLICE + sub64
        inside = jnp.where((first <= pos) & (pos < last), 1.0, 0.0)
        konehot[pl.ds(pl.multiple_of(s * SLICE, SLICE), SLICE), :] = inside.astype(jnp.bfloat16)
        return 0

    def mark(b):
        lax.fori_loop(8 * b, 8 * b + 8, key_marks, 0)

    def query_marks(i, _):
        owner, half, s = i // 8, lax.rem(i // 4, 2), lax.rem(i, 4)
        start = disp[(y * NX + ring(x, owner, NX)) * 8 + half * 4 + s] * SLICE
        for j in range(2):
            for p in range(2):
                pos = start + (j * 32 + p * 16) + sub16
                qbias[owner, p, half, 2 * s + j] = jnp.where(first > pos, HIDDEN, 0.0).astype(
                    jnp.bfloat16
                )
        return 0

    def turn(b):
        block = vbuf[b].reshape(512, HD).astype(jnp.float32)
        vt[:HD, b * 512 : (b + 1) * 512] = jnp.transpose(block).astype(jnp.bfloat16)

    vt[HD:, :] = jnp.ones((16, KEYS), jnp.bfloat16)

    lax.fori_loop(0, NX * 8, query_marks, 0)
    mark(0)
    for copy in swaps:
        copy.wait_recv()
    turn(0)

    def level_blocks(d):
        return (d,) if d in (0, 4) else (d, NY - d)

    def scores(d, owner, p, score, peak_ref):
        qa = jnp.concatenate(
            [qbuf[owner, p].reshape(ROWS, HD), qbias[owner, p].reshape(ROWS, HD)], axis=1
        )
        peak = None
        for i, b in enumerate(level_blocks(d)):
            ka = jnp.concatenate(
                [kbuf[b].reshape(512, HD), konehot[b * 512 : (b + 1) * 512, :]], axis=1
            )
            s = lax.dot_general(
                ka, qa, (((1,), (1,)), ((), ())), preferred_element_type=jnp.float32
            )
            score[i * 512 : (i + 1) * 512, :] = s
            tile = jnp.max(s.reshape(64, 8, ROWS), axis=0)
            peak = tile if peak is None else jnp.maximum(peak, tile)
            if b == level_blocks(d)[-1]:
                peak_ref[...] = jnp.broadcast_to(jnp.max(peak, axis=0, keepdims=True), (8, ROWS))
            yield

    def weigh(d, owner, p, score, peak_ref):
        peak = peak_ref[0:1, :]
        if d > 0:
            before = part_m[owner, p][0:1, :]
            peak = jnp.maximum(before, peak)
        total = None
        for i, b in enumerate(level_blocks(d)):
            w = jnp.exp2((score[i * 512 : (i + 1) * 512, :] - peak) * SCALE).astype(jnp.bfloat16)
            t = jnp.dot(
                vt[:, b * 512 : (b + 1) * 512], w, preferred_element_type=jnp.float32
            )
            total = t if total is None else total + t
            if b == level_blocks(d)[-1]:
                o, l = total[:HD, :], total[HD : HD + 1, :]
                if d > 0:
                    factor = jnp.exp2((before - peak) * SCALE)
                    o = part_o[owner, p] * factor + o
                    l = part_l[owner, p][0:1, :] * factor + l
                if d < 4 or owner == 0:
                    part_o[owner, p] = o
                    part_m[owner, p] = jnp.broadcast_to(peak, (8, ROWS))
                    part_l[owner, p] = jnp.broadcast_to(l, (8, ROWS))
                else:
                    give(owner, p, o, peak, l)
            yield

    def beside(*streams):
        live = list(streams)
        while live:
            live = [stream for stream in live if next(stream, True) is None]

    sub8 = lax.broadcasted_iota(jnp.int32, (8, ROWS), 0)
    given = {}

    def give(owner, p, o, peak, l):
        slot = 3 * p + owner - 1
        yo_send[slot] = o.astype(jnp.bfloat16)
        yl_send[slot] = jnp.where(sub8 < 4, peak, l)
        dev = x_dev(owner)
        given[slot] = (
            send(yo_send.at[slot], yo_recv.at[slot], yo_s.at[slot], yo_r.at[slot], dev),
            send(yl_send.at[slot], yl_recv.at[slot], yl_s.at[slot], yl_r.at[slot], dev),
        )

    buffers = ((score_a, peak_a), (score_b, peak_b))

    def stage(d, units, tasks, marks=(), ready=None):
        beside(scores(d, *units[0], *buffers[0]))
        if ready is not None:
            ready()
        for i, unit in enumerate(units):
            for task in tasks[i : i + 1]:
                arrive(*task)
            if i < len(marks):
                mark(marks[i])
            streams = [weigh(d, *unit, *buffers[i % 2])]
            if i + 1 < len(units):
                streams.insert(0, scores(d, *units[i + 1], *buffers[(i + 1) % 2]))
            beside(*streams)
        for task in tasks[len(units) :]:
            arrive(*task)

    order = [(owner, p) for owner in (2, 1, 3, 0) for p in range(2)]
    stage(0, order[6:], [])
    q_far = []
    for t in range(2):
        for p in range(2):
            q_hop[p, p][t].wait_recv()
            way = 1 - 2 * p
            slot = 8 + 2 * p + t
            q_far.append(
                send(
                    qbuf.at[-way % NX, p, halves[t]], qbuf.at[2, p, halves[t]],
                    q_s.at[slot], q_r.at[slot], x_dev(way),
                )
            )
    for task in arrivals(1)[:2]:
        arrive(*task)
    for p in range(2):
        for copy in q_hop[p, 1 - p]:
            copy.wait_recv()
    stage(0, order[2:6], arrivals(1)[2:])
    for copy in q_far:
        copy.wait_recv()
    stage(0, order[:2], [], (1, 7))
    for d in range(1, 3):
        turn(d)
        turn(NY - d)
        stage(d, order, arrivals(d + 1), (d + 1, NY - d - 1))
    turn(3)
    turn(5)
    stage(3, order, [], (4,))
    drain()
    for task in arrivals(4)[:2]:
        arrive(*task)

    def last_values():
        for task in arrivals(4)[2:]:
            arrive(*task)
        turn(4)

    stage(4, order[0::2][:3] + order[1::2][:3] + order[6:], [], ready=last_values)

    def finish(p):
        slots = [3 * p + k for k in range(3)]
        for slot in slots:
            for copy in given[slot]:
                copy.wait_recv()
        tops = [part_m[0, p][0:1, :]] + [yl_recv[slot][0:1, :] for slot in slots]
        sums = [part_l[0, p][0:1, :]] + [yl_recv[slot][4:5, :] for slot in slots]
        top = functools.reduce(jnp.maximum, tops)
        factors = [jnp.exp2((m - top) * SCALE) for m in tops]
        inverse = 1.0 / sum(f * l for f, l in zip(factors, sums))
        o = part_o[0, p] * (factors[0] * inverse)
        for f, slot in zip(factors[1:], slots):
            o = o + yo_recv[slot].astype(jnp.float32) * (f * inverse)
        o = jnp.transpose(o).astype(jnp.bfloat16)
        att_send[p] = jnp.where(c == 0, o[PIECE:], o[:PIECE])
        back = send(att_send.at[p], att.at[p, c], at_s.at[p], at_r.at[p], sibling)
        att[p, c] = jnp.where(c == 0, o[:PIECE], o[PIECE:])
        back.wait_recv()

    part = D // 4

    def project(p, h):
        rows = jnp.concatenate([att[p, 0], att[p, 1]], axis=1)

        cut = slice(h * part, (h + 1) * part)
        r = jnp.dot(rows, wbuf[:, cut], preferred_element_type=jnp.float32)
        proj[p, :, :, cut] = r.reshape(NZ, 16, part)

    zhops = {}

    def z_hop(j, p, short, h):
        travel = (2 * p - 1) * (1 - 2 * short) * (1 - 2 * (h % 2))
        owner = ring(z, travel * (5 - j - short), NZ)
        r = proj[p, owner, :, h * part : (h + 1) * part]
        slot = (4 * p + h) * 7 + 4 * short + j - 1
        if j > 1:
            zhops[slot - 1].wait_recv()
            r = r + z_recv[slot - 1].astype(jnp.float32)
        z_send[slot] = r.astype(jnp.bfloat16)
        zhops[slot] = send(
            z_send.at[slot], z_recv.at[slot], z_s.at[slot], z_r.at[slot], z_dev(travel)
        )

    load_w.wait()
    for p in range(2):
        finish(p)
        for h in range(4):
            project(p, h)
            for short in range(2):
                z_hop(1, p, short, h)
    for j in range(2, 5):
        if j == 3:
            drain()
        for p in range(2):
            for short in range(2 if j < 4 else 1):
                for h in range(4):
                    z_hop(j, p, short, h)
    for p in range(2):
        for h in range(4):
            r = proj[p, z, :, h * part : (h + 1) * part]
            for slot in ((4 * p + h) * 7 + 6, (4 * p + h) * 7 + 3):
                zhops[slot].wait_recv()
                r = r + z_recv[slot].astype(jnp.float32)
            out[p * 16 : (p + 1) * 16, h * part : (h + 1) * part] = r.astype(jnp.bfloat16)
    drain()


def body(queries, keys, values, group_lens, dispatch, out_weight):
    bf, f32 = jnp.bfloat16, jnp.float32
    dma = pltpu.SemaphoreType.DMA
    anywhere = pl.BlockSpec(memory_space=pl.ANY)
    return pl.pallas_call(
        kernel,
        out_shape=jax.ShapeDtypeStruct((ROWS // NZ, D), bf),
        in_specs=[anywhere] * 6,
        out_specs=pl.BlockSpec(memory_space=pltpu.VMEM),
        scratch_shapes=[
            pltpu.SMEM((32,), jnp.int32),
            pltpu.SMEM((256,), jnp.int32),
            pltpu.VMEM((NX, 2, 2, NZ, 16, HD), bf),
            pltpu.VMEM((NX, 2, 2, NZ, 16, HD), bf),
            pltpu.VMEM((NY, 2, ROWS, HD), bf),
            pltpu.VMEM((NY, 2, ROWS, HD), bf),
            pltpu.VMEM((HD + 16, KEYS), bf),
            pltpu.VMEM((KEYS, HD), bf),
            pltpu.VMEM((1024, ROWS), f32),
            pltpu.VMEM((1024, ROWS), f32),
            pltpu.VMEM((8, ROWS), f32),
            pltpu.VMEM((8, ROWS), f32),
            pltpu.VMEM((NX, 2, HD, ROWS), f32),
            pltpu.VMEM((NX, 2, 8, ROWS), f32),
            pltpu.VMEM((NX, 2, 8, ROWS), f32),
            pltpu.VMEM((6, HD, ROWS), bf),
            pltpu.VMEM((6, 8, ROWS), f32),
            pltpu.VMEM((6, HD, ROWS), bf),
            pltpu.VMEM((6, 8, ROWS), f32),
            pltpu.VMEM((2, 2, PIECE, HD), bf),
            pltpu.VMEM((2, PIECE, HD), bf),
            pltpu.VMEM((2 * HD, D), bf),
            pltpu.VMEM((2, NZ, 16, D), f32),
            pltpu.VMEM((56, 16, D // 4), bf),
            pltpu.VMEM((56, 16, D // 4), bf),
            dma((7,)), dma((4,)), dma((4,)), dma((12,)), dma((12,)), dma((28,)), dma((28,)),
            dma((6,)), dma((6,)), dma((6,)), dma((6,)), dma((2,)), dma((2,)),
            dma((56,)), dma((56,)),
        ],
        compiler_params=pltpu.CompilerParams(
            collective_id=0, has_side_effects=True, vmem_limit_bytes=60 * 1024 * 1024
        ),
        cost_estimate=pl.CostEstimate(
            flops=9_000_000_000, bytes_accessed=6_000_000, transcendentals=8_400_000
        ),
    )(
        group_lens,
        dispatch,
        queries.reshape(NZ, 2, 16, 2 * HD),
        keys,
        values,
        out_weight,
    )


def solution(mesh):
    return jax.shard_map(
        body,
        mesh=mesh,
        in_specs=(P("ctx", "head"), P("ctx", "head"), P("ctx", "head"), P(), P(), P("head", None)),
        out_specs=P(("ctx", "head"), None),
        check_vma=False,
    )
```
